32 devices in a mesh: adapter: 16 (over z, y, core), tensor: 2 (over x).
Axes of the slice: x: 2, y: 2, z: 4, core: 2. Of those that a mesh axis runs over, the one named last changes fastest.
Arguments:
- residual_rows: bfloat16 [12288, 8192], P(('adapter', 'tensor')), may hold values from -6 to 6
- norm_gain_vector: bfloat16 [8192], replicated, may hold values from 0.099609375 to 1.8984375
- key_value_weight: bfloat16 [8192, 2048], P(None, 'tensor'), may hold values from -0.0625 to 0.0625
- adapter_down_weight: bfloat16 [128, 8192, 64], P('adapter', 'tensor'), may hold values from -0.0625 to 0.0625
- adapter_up_weight: bfloat16 [128, 64, 1024], P('adapter', None, 'tensor'), may hold values from -0.375 to 0.375
- request_adapter_index: int32 [3072, 1], P('adapter'), may hold values from 0 to 127, as said below
Outputs:
- projected: bfloat16 [12288, 2048], P('adapter', 'tensor')
The draws below stay inside these ranges and needn't reach their ends.
Inputs may be any that keep to these rules, and one draw needn't show every extreme that they name: `request_adapter_index`: among the 192 requests of one index of adapter (aligned blocks of rows), no adapter is named more than 3 times and some adapter exactly 3 times; adapters a with the same a // 8 are named at most 12 times together, and some such set exactly 12 times.
All inputs are finite; a program needn't handle non-finite values.
Results may differ from the reference program's by a relative error of at most 0.0055.
Values may be sent and summed in bfloat16 or wider, within the bound.
No kernel may reach another device: no remote copies, remote signals or barrier semaphores. Data moves between devices by JAX's collectives and lax.ppermute only.
A program may use at most 128 MiB of HBM per device.

```python
import jax
import jax.numpy as jnp
from jax import lax

HIDDEN_WIDTH = 8192
KEY_VALUE_WIDTH = 1024
ADAPTER_RANK = 64
DRAFT = 4
REQ_G = 192
MOST = 3
DEST = 12
ADP_DEV = 8
ADAPTER_POOL = 128
REQUESTS = 3072
TOKENS = 12288
N_TENSOR = 2


def draw_request_adapter_index(key, part):
    key = jax.random.fold_in(key, 7)
    holders = ADAPTER_POOL // ADP_DEV
    slot_total = holders * DEST
    holder_order = jax.random.permutation(jax.random.fold_in(key, 1), holders)
    local_keys = jax.random.split(jax.random.fold_in(key, 2), holders)
    local_order = jax.vmap(lambda k: jax.random.permutation(k, ADP_DEV))(local_keys)

    def one_group(group):
        group_key = jax.random.fold_in(key, group + 100)
        position = jnp.arange(slot_total, dtype=jnp.int32)
        rank = position // DEST
        raw = jax.random.randint(jax.random.fold_in(group_key, 1), (slot_total,), 0, 4096)
        score = raw // (1 + rank) + jnp.where(rank == 0, 8192, 0)
        score = score * slot_total + (slot_total - 1 - position)
        unused, chosen = lax.top_k(score, REQ_G)
        holder = holder_order[chosen // DEST]
        local = local_order[holder, chosen % DEST // MOST]
        names = holder * ADP_DEV + local
        order = jax.random.permutation(jax.random.fold_in(group_key, 2), REQ_G)
        return names[order]
    result = jax.vmap(one_group)(jnp.arange(holders, dtype=jnp.int32))
    return result.reshape(-1, 1).astype(jnp.int32)


def level_of(own_key, extent, cuts, low, top_value):
    def one(axis_at, blocks):
        steps = jax.random.uniform(jax.random.fold_in(jax.random.fold_in(own_key, 6), axis_at), (blocks,), jnp.float32, low / len(cuts), top_value / len(cuts))
        return jnp.repeat(jnp.exp(steps), extent[axis_at] // blocks).reshape((-1,) + (1,) * (len(extent) - axis_at - 1))

    loudness = one(*cuts[0])
    for cut in cuts[1:]:
        loudness = loudness * one(*cut)
    return loudness


def gaussian(rng, dims, scale, reach, shards=(), kind=jnp.bfloat16):
    gain = level_of(rng, dims, shards, -0.22, 0.18) if shards else 1.0
    entries = jax.random.normal(rng, dims, jnp.float32) * scale * gain
    return jnp.minimum(jnp.maximum(entries, -reach), reach).astype(kind)


def setup_inputs(seed: int = 0) -> dict:
    splits = jax.random.split(jax.random.key(seed), 7)
    return {
        "residual_rows": gaussian(splits[0], (TOKENS, HIDDEN_WIDTH), 1.0, 6.0, ((0, 32),)),
        "norm_gain_vector": jnp.clip(1.0 + 0.18 * jax.random.normal(splits[1], (HIDDEN_WIDTH,), jnp.float32), 0.099609375, 1.8984375).astype(jnp.bfloat16),
        "key_value_weight": gaussian(splits[2], (HIDDEN_WIDTH, 2 * KEY_VALUE_WIDTH), HIDDEN_WIDTH ** -0.5, 0.0625, ((1, 2),)),
        "adapter_down_weight": gaussian(splits[3], (ADAPTER_POOL, HIDDEN_WIDTH, ADAPTER_RANK), HIDDEN_WIDTH ** -0.5, 0.0625, ((0, 16), (1, 2))),
        "adapter_up_weight": gaussian(splits[4], (ADAPTER_POOL, ADAPTER_RANK, KEY_VALUE_WIDTH), (4 * ADAPTER_RANK) ** -0.5, 0.375, ((0, 16), (2, 2))),
        "request_adapter_index": draw_request_adapter_index(jax.random.fold_in(splits[6], 71), 0),
    }


EPS = 1e-05
ADAPTER_SCALE = 2.0

def reference(residual_rows, norm_gain_vector, key_value_weight, adapter_down_weight, adapter_up_weight, request_adapter_index):
    values = residual_rows.astype(jnp.float32)
    inverse = lax.rsqrt(lax.optimization_barrier(jnp.mean(values * values, axis=-1, keepdims=True)) + EPS)
    normed = (values * inverse * norm_gain_vector.astype(jnp.float32)).astype(jnp.bfloat16)
    base = jnp.dot(normed, key_value_weight, preferred_element_type=jnp.float32)
    share = KEY_VALUE_WIDTH // N_TENSOR
    base = base.reshape(TOKENS, N_TENSOR, 2, share)
    grouped = normed.reshape(REQUESTS, DRAFT, HIDDEN_WIDTH)

    def per_request(item):
        rows, adapter_choice = item
        down_factor = adapter_down_weight[adapter_choice]
        up_factor = adapter_up_weight[adapter_choice]
        shrink_step = jnp.dot(rows, down_factor, preferred_element_type=jnp.float32).astype(jnp.bfloat16)
        return (jnp.dot(shrink_step, up_factor, preferred_element_type=jnp.float32) * ADAPTER_SCALE).astype(jnp.bfloat16)
    delta = lax.map(per_request, (grouped, request_adapter_index[:, 0]))
    delta = delta.reshape(TOKENS, N_TENSOR, share).astype(jnp.float32)
    keys = base[:, :, 0, :]
    vals = base[:, :, 1, :] + delta
    joined = jnp.stack([keys, vals], axis=2).astype(jnp.bfloat16)
    return joined.reshape(TOKENS, 2 * KEY_VALUE_WIDTH)
```

```python
import jax
import jax.numpy as jnp
from jax import lax
from jax.sharding import PartitionSpec as P

DRAFT = 4
DEST = 12


EPS = 1e-05
ADAPTER_SCALE = 2.0


def chunk_bounds(width):
    first = max(width // 8, 128)
    second = first + max(width // 4, 128)
    return [(0, first), (first, second), (second, width)]


def onehot(row_of_column, rows):
    row = lax.broadcasted_iota(jnp.int32, (rows, row_of_column.shape[0]), 0)
    return (row == row_of_column[None, :]).astype(jnp.bfloat16)


def features(rows, start, width):
    return lax.dynamic_slice_in_dim(rows, start, width, 1)


def per_device(
    residual_rows,
    norm_gain_vector,
    key_value_weight,
    adapter_down_weight,
    adapter_up_weight,
    request_adapter_index,
):
    tensor_count = lax.axis_size("tensor")
    tensor_index = lax.axis_index("tensor")
    adapter_count = lax.axis_size("adapter")
    adapter_index = lax.axis_index("adapter")
    own_tokens, model_width = residual_rows.shape
    share_width = model_width // tensor_count
    column_block_width = adapter_up_weight.shape[2]
    resident_adapters = adapter_down_weight.shape[0]
    rank_width = adapter_down_weight.shape[2]
    holder_slots = DEST * DRAFT
    slot_count = adapter_count * holder_slots
    offsets = range(1, tensor_count)

    def to_offset(value, offset):
        pairs = [(i, (i + offset) % tensor_count) for i in range(tensor_count)]
        return lax.ppermute(value, "tensor", pairs)

    request_ids = request_adapter_index[:, 0]
    request_count = request_ids.shape[0]
    holder = request_ids // resident_adapters
    position = lax.broadcasted_iota(jnp.int32, (request_count, request_count), 0)
    earlier = lax.broadcasted_iota(jnp.int32, (request_count, request_count), 1) < position
    same = holder[:, None] == holder[None, :]
    ranking = jnp.sum((same & earlier).astype(jnp.int32), axis=1)
    request_slot = holder * DEST + ranking
    draft_steps = jnp.arange(DRAFT, dtype=jnp.int32)[None, :]
    token_slot = (request_slot[:, None] * DRAFT + draft_steps).reshape(-1)

    slot = lax.broadcasted_iota(jnp.int32, (adapter_count * DEST, request_count), 0)
    hit = slot == request_slot[None, :]
    local = request_ids - holder * resident_adapters
    slot_local = jnp.sum(jnp.where(hit, local[None, :] + 1, 0), axis=1) - 1
    told = lax.all_gather(slot_local.reshape(adapter_count, DEST), "adapter", axis=0)
    told = lax.dynamic_index_in_dim(told, adapter_index, 1, keepdims=False)
    slot_adapter = jnp.repeat(told.reshape(-1), DRAFT)

    def owner_slots(offset):
        owner = (tensor_index - offset) % tensor_count
        return lax.dynamic_slice_in_dim(token_slot, owner * own_tokens, own_tokens, 0)

    place = [onehot(owner_slots(offset), slot_count) for offset in range(tensor_count)]

    scaled = (
        residual_rows.astype(jnp.float32) * norm_gain_vector.astype(jnp.float32)
    ).astype(jnp.bfloat16)

    down = jnp.swapaxes(adapter_down_weight, 1, 2).reshape(resident_adapters * rank_width, share_width)
    partial_value = jnp.zeros((resident_adapters * rank_width, slot_count), jnp.float32)
    others = [jnp.zeros((own_tokens, 2 * column_block_width), jnp.float32) for _ in offsets]
    own_start = tensor_index * share_width
    for low, high in chunk_bounds(share_width):
        width = high - low
        outgoing = jnp.dot(
            place[0], features(scaled, own_start + low, width), preferred_element_type=jnp.float32
        )
        for offset in offsets:
            target = (tensor_index + offset) % tensor_count
            piece = to_offset(features(scaled, target * share_width + low, width), offset)
            outgoing += jnp.dot(place[offset], piece, preferred_element_type=jnp.float32)
            others[offset - 1] += jnp.dot(
                piece,
                lax.dynamic_slice_in_dim(key_value_weight, own_start + low, width, 0),
                preferred_element_type=jnp.float32,
            )
        outgoing = outgoing.astype(jnp.bfloat16).reshape(adapter_count, holder_slots, width)
        received = lax.all_to_all(outgoing, "adapter", split_axis=0, concat_axis=0, tiled=True)
        partial_value += lax.dot_general(
            down[:, low:high],
            received.reshape(slot_count, width),
            (((1,), (1,)), ((), ())),
            preferred_element_type=jnp.float32,
        )

    for offset in offsets:
        target = (tensor_index + offset) % tensor_count
        rest = jnp.concatenate(
            [features(scaled, (target + j) % tensor_count * share_width, share_width) for j in offsets],
            axis=1,
        )
        rest = to_offset(rest, offset)
        for j in offsets:
            weight_rows = lax.dynamic_slice_in_dim(
                key_value_weight, (tensor_index + j) % tensor_count * share_width, share_width, 0
            )
            others[offset - 1] += jnp.dot(
                rest[:, (j - 1) * share_width : j * share_width],
                weight_rows,
                preferred_element_type=jnp.float32,
            )
    own = jnp.dot(scaled, key_value_weight, preferred_element_type=jnp.float32)

    values = residual_rows.astype(jnp.float32)
    inverse = lax.rsqrt(jnp.mean(values * values, axis=-1) + EPS)
    inverse = [inverse] + [to_offset(inverse, offset) for offset in offsets]

    partial_value = partial_value.reshape(resident_adapters, rank_width, slot_count)
    mine = jnp.arange(resident_adapters, dtype=jnp.int32)[:, None, None] == slot_adapter[None, None, :]
    partial_value = jnp.sum(jnp.where(mine, partial_value, 0.0), axis=0)
    total = partial_value
    for offset in offsets:
        total += to_offset(partial_value, offset)
    shrunk = total.astype(jnp.bfloat16)
    spread = jnp.where(mine, shrunk[None], jnp.zeros((), jnp.bfloat16))
    correction = lax.dot_general(
        spread.reshape(resident_adapters * rank_width, slot_count),
        adapter_up_weight.reshape(resident_adapters * rank_width, column_block_width),
        (((0,), (0,)), ((), ())),
        preferred_element_type=jnp.float32,
    )
    correction = (correction * ADAPTER_SCALE).astype(jnp.bfloat16)
    returned = lax.all_to_all(
        correction.reshape(adapter_count, holder_slots, column_block_width),
        "adapter",
        split_axis=0,
        concat_axis=0,
        tiled=True,
    ).reshape(slot_count, column_block_width)

    result = jnp.zeros((own_tokens * tensor_count, 2 * column_block_width), jnp.bfloat16)
    for offset, base in enumerate([own] + others):
        delta = lax.dot_general(
            place[offset], returned, (((0,), (0,)), ((), ())), preferred_element_type=jnp.float32
        )
        keys = base[:, :column_block_width]
        vals = base[:, column_block_width:] + delta
        rows = (jnp.concatenate([keys, vals], axis=1) * inverse[offset][:, None]).astype(jnp.bfloat16)
        owner = (tensor_index - offset) % tensor_count
        result = lax.dynamic_update_slice_in_dim(result, rows, owner * own_tokens, 0)
    return result


def solution(mesh):
    in_specs = (
        P(("adapter", "tensor"), None),
        P(),
        P(None, "tensor"),
        P("adapter", "tensor", None),
        P("adapter", None, "tensor"),
        P("adapter", None),
    )
    out_specs = P("adapter", "tensor")
    return jax.shard_map(
        per_device, mesh=mesh, in_specs=in_specs, out_specs=out_specs, check_vma=False
    )
```

```python
import jax
import jax.numpy as jnp
from jax import lax
from jax.sharding import PartitionSpec as P

DRAFT = 4
DEST = 12


EPS = 1e-05
ADAPTER_SCALE = 2.0


def chunk_bounds(width):
    first = max(width // 8, 128)
    second = first + max(width // 4, 128)
    return [(0, first), (first, second), (second, width)]


def onehot(row_of_column, rows):
    row = lax.broadcasted_iota(jnp.int32, (rows, row_of_column.shape[0]), 0)
    return (row == row_of_column[None, :]).astype(jnp.bfloat16)


def features(rows, start, width):
    return lax.dynamic_slice_in_dim(rows, start, width, 1)


def per_device(
    residual_rows,
    norm_gain_vector,
    key_value_weight,
    adapter_down_weight,
    adapter_up_weight,
    request_adapter_index,
):
    tensor_count = lax.axis_size("tensor")
    tensor_index = lax.axis_index("tensor")
    adapter_count = lax.axis_size("adapter")
    adapter_index = lax.axis_index("adapter")
    own_tokens, model_width = residual_rows.shape
    share_width = model_width // tensor_count
    column_block_width = adapter_up_weight.shape[2]
    resident_adapters = adapter_down_weight.shape[0]
    rank_width = adapter_down_weight.shape[2]
    holder_slots = DEST * DRAFT
    slot_count = adapter_count * holder_slots
    offsets = range(1, tensor_count)

    def to_offset(value, offset):
        pairs = [(i, (i + offset) % tensor_count) for i in range(tensor_count)]
        return lax.ppermute(value, "tensor", pairs)

    request_ids = request_adapter_index[:, 0]
    request_count = request_ids.shape[0]
    holder = request_ids // resident_adapters
    position = lax.broadcasted_iota(jnp.int32, (request_count, request_count), 0)
    earlier = lax.broadcasted_iota(jnp.int32, (request_count, request_count), 1) < position
    same = holder[:, None] == holder[None, :]
    ranking = jnp.sum((same & earlier).astype(jnp.int32), axis=1)
    request_slot = holder * DEST + ranking
    draft_steps = jnp.arange(DRAFT, dtype=jnp.int32)[None, :]
    token_slot = (request_slot[:, None] * DRAFT + draft_steps).reshape(-1)

    slot = lax.broadcasted_iota(jnp.int32, (adapter_count * DEST, request_count), 0)
    hit = slot == request_slot[None, :]
    local = request_ids - holder * resident_adapters
    slot_local = jnp.sum(jnp.where(hit, local[None, :] + 1, 0), axis=1) - 1
    told = lax.all_to_all(
        slot_local.reshape(adapter_count, DEST), "adapter", split_axis=0, concat_axis=0, tiled=True
    )
    slot_adapter = jnp.repeat(told.reshape(-1), DRAFT)

    def owner_slots(offset):
        owner = (tensor_index - offset) % tensor_count
        return lax.dynamic_slice_in_dim(token_slot, owner * own_tokens, own_tokens, 0)

    place = [onehot(owner_slots(offset), slot_count) for offset in range(tensor_count)]

    def scaled(rows, start, width):
        gain = lax.dynamic_slice_in_dim(norm_gain_vector, start, width, 0).astype(jnp.float32)
        return (features(rows, start, width).astype(jnp.float32) * gain).astype(jnp.bfloat16)

    down = jnp.swapaxes(adapter_down_weight, 1, 2).reshape(resident_adapters * rank_width, share_width)
    partial_value = jnp.zeros((resident_adapters * rank_width, slot_count), jnp.float32)
    others = [jnp.zeros((own_tokens, 2 * column_block_width), jnp.float32) for _ in offsets]
    own_start = tensor_index * share_width
    source = residual_rows
    sent = told
    for low, high in chunk_bounds(share_width):
        width = high - low
        pieces = [
            to_offset(
                scaled(source, (tensor_index + offset) % tensor_count * share_width + low, width), offset
            )
            for offset in offsets
        ]
        outgoing = jnp.dot(
            place[0], scaled(source, own_start + low, width), preferred_element_type=jnp.float32
        )
        source, *pieces = lax.optimization_barrier((source, *pieces))
        for offset, piece in zip(offsets, pieces):
            outgoing += jnp.dot(place[offset], piece, preferred_element_type=jnp.float32)
            others[offset - 1] += jnp.dot(
                piece,
                lax.dynamic_slice_in_dim(key_value_weight, own_start + low, width, 0),
                preferred_element_type=jnp.float32,
            )
        outgoing = outgoing.astype(jnp.bfloat16).reshape(adapter_count, holder_slots, width)
        outgoing, sent = lax.optimization_barrier((outgoing, sent))
        sent = lax.all_to_all(outgoing, "adapter", split_axis=0, concat_axis=0, tiled=True)
        partial_value += lax.dot_general(
            down[:, low:high],
            sent.reshape(slot_count, width),
            (((1,), (1,)), ((), ())),
            preferred_element_type=jnp.float32,
        )

    for offset in offsets:
        target = (tensor_index + offset) % tensor_count
        rest = jnp.concatenate(
            [scaled(source, (target + j) % tensor_count * share_width, share_width) for j in offsets],
            axis=1,
        )
        rest = to_offset(rest, offset)
        for j in offsets:
            weight_rows = lax.dynamic_slice_in_dim(
                key_value_weight, (tensor_index + j) % tensor_count * share_width, share_width, 0
            )
            others[offset - 1] += jnp.dot(
                rest[:, (j - 1) * share_width : j * share_width],
                weight_rows,
                preferred_element_type=jnp.float32,
            )
    own = jnp.dot(
        scaled(source, 0, model_width), key_value_weight, preferred_element_type=jnp.float32
    )

    values = source.astype(jnp.float32)
    inverse = lax.rsqrt(jnp.mean(values * values, axis=-1) + EPS)
    inverse = [inverse] + [to_offset(inverse, offset) for offset in offsets]

    partial_value = partial_value.reshape(resident_adapters, rank_width, slot_count)
    mine = jnp.arange(resident_adapters, dtype=jnp.int32)[:, None, None] == slot_adapter[None, None, :]
    partial_value = jnp.sum(jnp.where(mine, partial_value, 0.0), axis=0)
    total = partial_value
    for offset in offsets:
        total += to_offset(partial_value, offset)
    shrunk = total.astype(jnp.bfloat16)
    spread = jnp.where(mine, shrunk[None], jnp.zeros((), jnp.bfloat16))
    correction = lax.dot_general(
        spread.reshape(resident_adapters * rank_width, slot_count),
        adapter_up_weight.reshape(resident_adapters * rank_width, column_block_width),
        (((0,), (0,)), ((), ())),
        preferred_element_type=jnp.float32,
    )
    correction = (correction * ADAPTER_SCALE).astype(jnp.bfloat16)
    returned = lax.all_to_all(
        correction.reshape(adapter_count, holder_slots, column_block_width),
        "adapter",
        split_axis=0,
        concat_axis=0,
        tiled=True,
    ).reshape(slot_count, column_block_width)

    result = jnp.zeros((own_tokens * tensor_count, 2 * column_block_width), jnp.bfloat16)
    for offset, base in enumerate([own] + others):
        delta = lax.dot_general(
            place[offset], returned, (((0,), (0,)), ((), ())), preferred_element_type=jnp.float32
        )
        keys = base[:, :column_block_width]
        vals = base[:, column_block_width:] + delta
        rows = (jnp.concatenate([keys, vals], axis=1) * inverse[offset][:, None]).astype(jnp.bfloat16)
        owner = (tensor_index - offset) % tensor_count
        result = lax.dynamic_update_slice_in_dim(result, rows, owner * own_tokens, 0)
    return result


def solution(mesh):
    in_specs = (
        P(("adapter", "tensor"), None),
        P(),
        P(None, "tensor"),
        P("adapter", "tensor", None),
        P("adapter", None, "tensor"),
        P("adapter", None),
    )
    out_specs = P("adapter", "tensor")
    return jax.shard_map(
        per_device, mesh=mesh, in_specs=in_specs, out_specs=out_specs, check_vma=False
    )
```

```python
import functools

import jax
import jax.numpy as jnp
from jax import lax
from jax.experimental import pallas as pl
from jax.experimental.pallas import tpu as pltpu
from jax.sharding import PartitionSpec as P

DRAFT = 4
DEST = 12


EPS = 1e-05
ADAPTER_SCALE = 2.0


def chunk_bounds(width):
    first = max(width * 7 // 32 // 128, 1) * 128
    second = first + max(width * 5 // 16 // 128, 1) * 128
    return [(0, first), (first, second), (second, width)]


def after(value, *earlier):
    return lax.optimization_barrier((value, *earlier))[0]


def onehot(row_of_column, rows):
    row = lax.broadcasted_iota(jnp.int32, (rows, row_of_column.shape[0]), 0)
    return (row == row_of_column[None, :]).astype(jnp.bfloat16)


def features(rows, start, width):
    return lax.dynamic_slice_in_dim(rows, start, width, 1)


def shrink_kernel(adapters, down_ref, sent_ref, earlier_ref, slot_adapter_ref, out_ref):
    rank_width, slots = out_ref.shape
    step = 256 if slots % 256 == 0 else slots
    for start in range(0, slots, step):
        columns = slice(start, start + step)
        partial_value = earlier_ref[:, columns] + lax.dot_general(
            down_ref[...],
            sent_ref[columns, :],
            (((1,), (1,)), ((), ())),
            preferred_element_type=jnp.float32,
        )
        named = slot_adapter_ref[:, columns]
        chosen = jnp.zeros((rank_width, step), jnp.float32)
        for adapter in range(adapters):
            rows = partial_value[adapter * rank_width : (adapter + 1) * rank_width]
            chosen = jnp.where(named == adapter, rows, chosen)
        out_ref[:, columns] = chosen


def shrink_last(down, sent, earlier, slot_adapter, adapters):
    rows, width = down.shape
    slots = sent.shape[0]
    return pl.pallas_call(
        functools.partial(shrink_kernel, adapters),
        out_shape=jax.ShapeDtypeStruct((rows // adapters, slots), jnp.float32),
        in_specs=[pl.BlockSpec(memory_space=pltpu.VMEM)] * 4,
        out_specs=pl.BlockSpec(memory_space=pltpu.VMEM),
        compiler_params=pltpu.CompilerParams(vmem_limit_bytes=16 * 1024 * 1024),
        cost_estimate=pl.CostEstimate(
            flops=2 * rows * width * slots,
            bytes_accessed=(rows + slots) * width * 2 + rows * slots * 4,
            transcendentals=0,
        ),
    )(down, sent, earlier, slot_adapter)


def finish_kernel(count, owners_ref, *refs):
    slots, factors, bases = refs[:count], refs[count : 2 * count], refs[2 * count : 3 * count]
    returned_ref, out_ref = refs[3 * count :]
    rows, width = bases[0].shape
    half = width // 2
    for i in range(count):
        slot = lax.broadcasted_iota(jnp.int32, (rows, returned_ref.shape[0]), 1)
        take = jnp.where(slot == slots[i][...], 1.0, 0.0).astype(jnp.bfloat16)
        delta = jnp.dot(take, returned_ref[...], preferred_element_type=jnp.float32)
        factor = factors[i][...]
        place = pl.ds(pl.multiple_of(owners_ref[i] * rows, rows), rows)
        out_ref[place, :half] = (bases[i][:, :half] * factor).astype(out_ref.dtype)
        out_ref[place, half:] = ((bases[i][:, half:] + delta) * factor).astype(out_ref.dtype)


def finish(owners, slots, factors, bases, returned):
    count = len(bases)
    rows, width = bases[0].shape
    return pl.pallas_call(
        functools.partial(finish_kernel, count),
        out_shape=jax.ShapeDtypeStruct((rows * count, width), jnp.bfloat16),
        in_specs=[pl.BlockSpec(memory_space=pltpu.SMEM)]
        + [pl.BlockSpec(memory_space=pltpu.VMEM)] * (3 * count + 1),
        out_specs=pl.BlockSpec(memory_space=pltpu.VMEM),
        compiler_params=pltpu.CompilerParams(vmem_limit_bytes=16 * 1024 * 1024),
        cost_estimate=pl.CostEstimate(
            flops=2 * rows * count * returned.shape[0] * returned.shape[1],
            bytes_accessed=rows * count * width * 6 + returned.size * 2,
            transcendentals=0,
        ),
    )(owners, *slots, *factors, *bases, returned)


def per_device(
    residual_rows,
    norm_gain_vector,
    key_value_weight,
    adapter_down_weight,
    adapter_up_weight,
    request_adapter_index,
):
    tensor_count = lax.axis_size("tensor")
    tensor_index = lax.axis_index("tensor")
    adapter_count = lax.axis_size("adapter")
    adapter_index = lax.axis_index("adapter")
    own_tokens, model_width = residual_rows.shape
    share_width = model_width // tensor_count
    column_block_width = adapter_up_weight.shape[2]
    resident_adapters = adapter_down_weight.shape[0]
    rank_width = adapter_down_weight.shape[2]
    holder_slots = DEST * DRAFT
    slot_count = adapter_count * holder_slots
    offsets = range(1, tensor_count)

    def to_offset(value, offset):
        pairs = [(i, (i + offset) % tensor_count) for i in range(tensor_count)]
        return lax.ppermute(value, "tensor", pairs)

    request_ids = request_adapter_index[:, 0]
    request_count = request_ids.shape[0]
    holder = request_ids // resident_adapters
    position = lax.broadcasted_iota(jnp.int32, (request_count, request_count), 0)
    earlier = lax.broadcasted_iota(jnp.int32, (request_count, request_count), 1) < position
    same = holder[:, None] == holder[None, :]
    ranking = jnp.sum((same & earlier).astype(jnp.int32), axis=1)
    request_slot = holder * DEST + ranking
    draft_steps = jnp.arange(DRAFT, dtype=jnp.int32)[None, :]
    token_slot = (request_slot[:, None] * DRAFT + draft_steps).reshape(-1)

    slot = lax.broadcasted_iota(jnp.int32, (adapter_count * DEST, request_count), 0)
    hit = slot == request_slot[None, :]
    local = request_ids - holder * resident_adapters
    slot_local = jnp.sum(jnp.where(hit, local[None, :] + 1, 0), axis=1) - 1
    told = lax.all_to_all(
        slot_local.reshape(adapter_count, DEST), "adapter", split_axis=0, concat_axis=0, tiled=True
    )
    slot_adapter = jnp.repeat(told.reshape(-1), DRAFT)

    def owner_slots(offset):
        owner = (tensor_index - offset) % tensor_count
        return lax.dynamic_slice_in_dim(token_slot, owner * own_tokens, own_tokens, 0)

    place = [onehot(owner_slots(offset), slot_count) for offset in range(tensor_count)]

    def scaled(rows, start, width):
        gain = lax.dynamic_slice_in_dim(norm_gain_vector, start, width, 0).astype(jnp.float32)
        return (features(rows, start, width).astype(jnp.float32) * gain).astype(jnp.bfloat16)

    down = jnp.swapaxes(adapter_down_weight, 1, 2).reshape(resident_adapters * rank_width, share_width)
    others = [jnp.zeros((own_tokens, 2 * column_block_width), jnp.float32) for _ in offsets]
    own_start = tensor_index * share_width
    bounds = chunk_bounds(share_width)

    def to_send(rows, low, width):
        starts = [(tensor_index + offset) % tensor_count * share_width + low for offset in offsets]
        return [scaled(rows, start, width) for start in starts]

    def rest_of(offset):
        target = (tensor_index + offset) % tensor_count
        rest = [scaled(later_rows, (target + j) % tensor_count * share_width, share_width) for j in offsets]
        starts = [(tensor_index + j) % tensor_count * share_width for j in offsets]
        weight_rows = [
            lax.dynamic_slice_in_dim(key_value_weight, start, share_width, 0) for start in starts
        ]
        return jnp.concatenate(rest, axis=1), jnp.concatenate(weight_rows, axis=0)

    later_rows = after(residual_rows, slot_local)
    parts = len(bounds)
    rest_width = model_width - share_width
    rest_cut = max(rest_width * 3 // 4 // 128, 1) * 128
    rests = [rest_of(offset) for offset in offsets]
    sending = [
        to_send(residual_rows if part == 0 else later_rows, low, high - low)
        for part, (low, high) in enumerate(bounds)
    ]
    sending.append([rest[:, :rest_cut] for rest, _ in rests])
    own, inverse = None, []
    partials = []
    for part, (low, high) in enumerate(bounds):
        width = high - low
        pieces = [to_offset(piece, offset) for offset, piece in zip(offsets, sending[part])]
        outgoing = jnp.dot(
            place[0],
            scaled(residual_rows if part == 0 else later_rows, own_start + low, width),
            preferred_element_type=jnp.float32,
        ).astype(jnp.bfloat16)
        if part == 0:
            meanwhile = [told]
        elif part == 1:
            values = after(later_rows, *gate).astype(jnp.float32)
            inverse = [lax.rsqrt(jnp.mean(values * values, axis=-1) + EPS)]
            inverse += [to_offset(inverse[0], offset) for offset in offsets]
            meanwhile = [*others, inverse[0]]
        else:
            own = jnp.dot(
                scaled(after(later_rows, *gate), 0, model_width),
                key_value_weight,
                preferred_element_type=jnp.float32,
            )
            meanwhile = [*others, own, *inverse[1:]]
        count = len(offsets)
        tied = lax.optimization_barrier((*pieces, *sending[part + 1], outgoing, *meanwhile))
        pieces, sending[part + 1] = tied[:count], tied[count : 2 * count]
        gate = pieces
        outgoing = tied[2 * count].astype(jnp.float32)
        if part == 1:
            others = list(tied[2 * count + 1 : 3 * count + 1])
        elif part > 1:
            others = list(tied[2 * count + 1 : 3 * count + 1])
            own = tied[3 * count + 1]
        for offset, piece in zip(offsets, pieces):
            outgoing += jnp.dot(place[offset], piece, preferred_element_type=jnp.float32)
            others[offset - 1] += jnp.dot(
                piece,
                lax.dynamic_slice_in_dim(key_value_weight, own_start + low, width, 0),
                preferred_element_type=jnp.float32,
            )
        outgoing = outgoing.astype(jnp.bfloat16).reshape(adapter_count, holder_slots, width)
        sent = lax.all_to_all(outgoing, "adapter", split_axis=0, concat_axis=0, tiled=True)
        sent = sent.reshape(slot_count, width)
        if part < parts - 1:
            if partials:
                sent = after(sent, partials[-1])
            partial_value = lax.dot_general(
                down[:, low:high], sent, (((1,), (1,)), ((), ())), preferred_element_type=jnp.float32
            )
            partials.append(partial_value + partials[-1] if partials else partial_value)

    early = [to_offset(piece, offset) for offset, piece in zip(offsets, sending[parts])]
    low, high = bounds[-1]
    sent, earlier_sum, last_down, *tied = lax.optimization_barrier(
        (sent, partials[-1], down[:, low:high], *others, *early)
    )
    others, early = tied[: len(offsets)], tied[len(offsets) :]
    partial_value = shrink_last(last_down, sent, earlier_sum, slot_adapter[None, :], resident_adapters)
    total = partial_value
    for offset in offsets:
        total += to_offset(partial_value, offset)

    for offset in offsets:
        rest, weight_rows = rests[offset - 1]
        late = to_offset(after(rest[:, rest_cut:], total), offset)
        for piece, piece_rows in (
            (early[offset - 1], weight_rows[:rest_cut]),
            (late, weight_rows[rest_cut:]),
        ):
            others[offset - 1] += jnp.dot(piece, piece_rows, preferred_element_type=jnp.float32)

    mine = jnp.arange(resident_adapters, dtype=jnp.int32)[:, None, None] == slot_adapter[None, None, :]
    shrunk = total.astype(jnp.bfloat16)
    spread = jnp.where(mine, shrunk[None], jnp.zeros((), jnp.bfloat16))
    correction = lax.dot_general(
        spread.reshape(resident_adapters * rank_width, slot_count),
        adapter_up_weight.reshape(resident_adapters * rank_width, column_block_width),
        (((0,), (0,)), ((), ())),
        preferred_element_type=jnp.float32,
    )
    correction = (correction * ADAPTER_SCALE).astype(jnp.bfloat16)
    returned = lax.all_to_all(
        correction.reshape(adapter_count, holder_slots, column_block_width),
        "adapter",
        split_axis=0,
        concat_axis=0,
        tiled=True,
    ).reshape(slot_count, column_block_width)

    owners = [(tensor_index - offset) % tensor_count for offset in range(tensor_count)]
    return finish(
        jnp.stack(owners).astype(jnp.int32),
        [owner_slots(offset)[:, None] for offset in range(tensor_count)],
        [column[:, None] for column in inverse],
        [own] + others,
        returned,
    )


def solution(mesh):
    in_specs = (
        P(("adapter", "tensor"), None),
        P(),
        P(None, "tensor"),
        P("adapter", "tensor", None),
        P("adapter", None, "tensor"),
        P("adapter", None),
    )
    out_specs = P("adapter", "tensor")
    return jax.shard_map(
        per_device, mesh=mesh, in_specs=in_specs, out_specs=out_specs, check_vma=False
    )
```

```python
import functools

import jax
import jax.numpy as jnp
from jax import lax
from jax.experimental import pallas as pl
from jax.experimental.pallas import tpu as pltpu
from jax.sharding import PartitionSpec as P

DRAFT = 4
DEST = 12


EPS = 1e-05
ADAPTER_SCALE = 2.0


def chunk_bounds(width):
    first = max(width * 7 // 32 // 128, 1) * 128
    second = first + max(width * 5 // 16 // 128, 1) * 128
    return [(0, first), (first, second), (second, width)]


def after(value, *earlier):
    return lax.optimization_barrier((value, *earlier))[0]


def onehot(row_of_column, rows):
    row = lax.broadcasted_iota(jnp.int32, (rows, row_of_column.shape[0]), 0)
    return (row == row_of_column[None, :]).astype(jnp.bfloat16)


def features(rows, start, width):
    return lax.dynamic_slice_in_dim(rows, start, width, 1)


def shrink_kernel(adapters, down_ref, sent_ref, earlier_ref, slot_adapter_ref, out_ref):
    rank_width, slots = out_ref.shape
    step = 256 if slots % 256 == 0 else slots
    for start in range(0, slots, step):
        columns = slice(start, start + step)
        partial_value = earlier_ref[:, columns] + lax.dot_general(
            down_ref[...],
            sent_ref[columns, :],
            (((1,), (1,)), ((), ())),
            preferred_element_type=jnp.float32,
        )
        named = slot_adapter_ref[:, columns]
        chosen = jnp.zeros((rank_width, step), jnp.float32)
        for adapter in range(adapters):
            rows = partial_value[adapter * rank_width : (adapter + 1) * rank_width]
            chosen = jnp.where(named == adapter, rows, chosen)
        out_ref[:, columns] = chosen


def shrink_last(down, sent, earlier, slot_adapter, adapters):
    rows, width = down.shape
    slots = sent.shape[0]
    return pl.pallas_call(
        functools.partial(shrink_kernel, adapters),
        out_shape=jax.ShapeDtypeStruct((rows // adapters, slots), jnp.float32),
        in_specs=[pl.BlockSpec(memory_space=pltpu.VMEM)] * 4,
        out_specs=pl.BlockSpec(memory_space=pltpu.VMEM),
        compiler_params=pltpu.CompilerParams(vmem_limit_bytes=16 * 1024 * 1024),
        cost_estimate=pl.CostEstimate(
            flops=2 * rows * width * slots,
            bytes_accessed=(rows + slots) * width * 2 + rows * slots * 4,
            transcendentals=0,
        ),
    )(down, sent, earlier, slot_adapter)


def finish_kernel(count, owners_ref, *refs):
    slots, factors, bases = refs[:count], refs[count : 2 * count], refs[2 * count : 3 * count]
    returned_ref, out_ref = refs[3 * count :]
    rows, width = bases[0].shape
    half = width // 2
    for i in range(count):
        slot = lax.broadcasted_iota(jnp.int32, (rows, returned_ref.shape[0]), 1)
        take = jnp.where(slot == slots[i][...], 1.0, 0.0).astype(jnp.bfloat16)
        delta = jnp.dot(take, returned_ref[...], preferred_element_type=jnp.float32)
        factor = factors[i][...]
        place = pl.ds(pl.multiple_of(owners_ref[i] * rows, rows), rows)
        out_ref[place, :half] = (bases[i][:, :half] * factor).astype(out_ref.dtype)
        out_ref[place, half:] = ((bases[i][:, half:] + delta) * factor).astype(out_ref.dtype)


def finish(owners, slots, factors, bases, returned):
    count = len(bases)
    rows, width = bases[0].shape
    return pl.pallas_call(
        functools.partial(finish_kernel, count),
        out_shape=jax.ShapeDtypeStruct((rows * count, width), jnp.bfloat16),
        in_specs=[pl.BlockSpec(memory_space=pltpu.SMEM)]
        + [pl.BlockSpec(memory_space=pltpu.VMEM)] * (3 * count + 1),
        out_specs=pl.BlockSpec(memory_space=pltpu.VMEM),
        compiler_params=pltpu.CompilerParams(vmem_limit_bytes=16 * 1024 * 1024),
        cost_estimate=pl.CostEstimate(
            flops=2 * rows * count * returned.shape[0] * returned.shape[1],
            bytes_accessed=rows * count * width * 6 + returned.size * 2,
            transcendentals=0,
        ),
    )(owners, *slots, *factors, *bases, returned)


def per_device(
    residual_rows,
    norm_gain_vector,
    key_value_weight,
    adapter_down_weight,
    adapter_up_weight,
    request_adapter_index,
):
    tensor_count = lax.axis_size("tensor")
    tensor_index = lax.axis_index("tensor")
    adapter_count = lax.axis_size("adapter")
    adapter_index = lax.axis_index("adapter")
    own_tokens, model_width = residual_rows.shape
    share_width = model_width // tensor_count
    column_block_width = adapter_up_weight.shape[2]
    resident_adapters = adapter_down_weight.shape[0]
    rank_width = adapter_down_weight.shape[2]
    holder_slots = DEST * DRAFT
    slot_count = adapter_count * holder_slots
    offsets = range(1, tensor_count)

    def to_offset(value, offset):
        pairs = [(i, (i + offset) % tensor_count) for i in range(tensor_count)]
        return lax.ppermute(value, "tensor", pairs)

    request_ids = request_adapter_index[:, 0]
    request_count = request_ids.shape[0]
    holder = request_ids // resident_adapters
    position = lax.broadcasted_iota(jnp.int32, (request_count, request_count), 0)
    earlier = lax.broadcasted_iota(jnp.int32, (request_count, request_count), 1) < position
    same = holder[:, None] == holder[None, :]
    ranking = jnp.sum((same & earlier).astype(jnp.int32), axis=1)
    request_slot = holder * DEST + ranking
    draft_steps = jnp.arange(DRAFT, dtype=jnp.int32)[None, :]
    token_slot = (request_slot[:, None] * DRAFT + draft_steps).reshape(-1)

    slot = lax.broadcasted_iota(jnp.int32, (adapter_count * DEST, request_count), 0)
    hit = slot == request_slot[None, :]
    local = request_ids - holder * resident_adapters
    slot_local = jnp.sum(jnp.where(hit, local[None, :] + 1, 0), axis=1) - 1
    told = lax.all_to_all(
        slot_local.reshape(adapter_count, DEST), "adapter", split_axis=0, concat_axis=0, tiled=True
    )
    slot_adapter = jnp.repeat(told.reshape(-1), DRAFT)

    def owner_slots(offset):
        owner = (tensor_index - offset) % tensor_count
        return lax.dynamic_slice_in_dim(token_slot, owner * own_tokens, own_tokens, 0)

    place = [onehot(owner_slots(offset), slot_count) for offset in range(tensor_count)]

    def scaled(rows, start, width):
        gain = lax.dynamic_slice_in_dim(norm_gain_vector, start, width, 0).astype(jnp.float32)
        return (features(rows, start, width).astype(jnp.float32) * gain).astype(jnp.bfloat16)

    down = jnp.swapaxes(adapter_down_weight, 1, 2).reshape(resident_adapters * rank_width, share_width)
    others = [jnp.zeros((own_tokens, 2 * column_block_width), jnp.float32) for _ in offsets]
    own_start = tensor_index * share_width
    bounds = chunk_bounds(share_width)

    def to_send(rows, low, width):
        starts = [(tensor_index + offset) % tensor_count * share_width + low for offset in offsets]
        return [scaled(rows, start, width) for start in starts]

    def rest_of(offset, rows):
        target = (tensor_index + offset) % tensor_count
        rest = [scaled(rows, (target + j) % tensor_count * share_width, share_width) for j in offsets]
        return jnp.concatenate(rest, axis=1)

    def rest_weight():
        starts = [(tensor_index + j) % tensor_count * share_width for j in offsets]
        return jnp.concatenate(
            [lax.dynamic_slice_in_dim(key_value_weight, start, share_width, 0) for start in starts], axis=0
        )

    def own_product(rows, low, high):
        return jnp.dot(
            scaled(rows, low, high - low), key_value_weight[low:high], preferred_element_type=jnp.float32
        )

    later_rows = after(residual_rows, slot_local)
    parts = len(bounds)
    rest_width = model_width - share_width
    rest_cut = max(rest_width * 13 // 16 // 128, 1) * 128
    sending = [
        to_send(residual_rows if part == 0 else later_rows, low, high - low)
        for part, (low, high) in enumerate(bounds)
    ]
    own, inverse, gate = None, [], ()
    partials = []
    for part, (low, high) in enumerate(bounds):
        width = high - low
        sending[part] = [after(piece, *gate) for piece in sending[part]]
        pieces = [to_offset(piece, offset) for offset, piece in zip(offsets, sending[part])]
        outgoing = jnp.dot(
            place[0],
            scaled(residual_rows if part == 0 else later_rows, own_start + low, width),
            preferred_element_type=jnp.float32,
        ).astype(jnp.bfloat16)
        outgoing = lax.optimization_barrier(outgoing).astype(jnp.float32)
        if part == 0:
            pieces = [after(piece, told) for piece in pieces]
        elif part == 1:
            values = after(later_rows, *gate).astype(jnp.float32)
            inverse = [lax.rsqrt(jnp.mean(values * values, axis=-1) + EPS)]
            inverse += [to_offset(inverse[0], offset) for offset in offsets]
            pieces = [after(piece, inverse[0]) for piece in pieces]
        else:
            own = own_product(after(later_rows, *gate), 0, model_width // 2)
            own, *pieces = lax.optimization_barrier((own, *pieces))
        gate = pieces
        for offset, piece in zip(offsets, pieces):
            outgoing += jnp.dot(place[offset], piece, preferred_element_type=jnp.float32)
            others[offset - 1] += jnp.dot(
                piece,
                lax.dynamic_slice_in_dim(key_value_weight, own_start + low, width, 0),
                preferred_element_type=jnp.float32,
            )
        outgoing = outgoing.astype(jnp.bfloat16).reshape(adapter_count, holder_slots, width)
        sent = lax.all_to_all(outgoing, "adapter", split_axis=0, concat_axis=0, tiled=True)
        sent = sent.reshape(slot_count, width)
        if part < parts - 1:
            if partials:
                sent = after(sent, partials[-1])
            partial_value = lax.dot_general(
                down[:, low:high], sent, (((1,), (1,)), ((), ())), preferred_element_type=jnp.float32
            )
            partials.append(partial_value + partials[-1] if partials else partial_value)

    early = [
        to_offset(after(rest_of(offset, later_rows)[:, :rest_cut], *gate), offset) for offset in offsets
    ]
    low, high = bounds[-1]
    sent, earlier_sum, last_down, *tied = lax.optimization_barrier(
        (sent, partials[-1], down[:, low:high], *others, *inverse[1:], *early)
    )
    count = len(offsets)
    others, inverse[1:], early = tied[:count], tied[count : 2 * count], tied[2 * count :]
    partial_value = shrink_last(last_down, sent, earlier_sum, slot_adapter[None, :], resident_adapters)
    total = partial_value
    for offset in offsets:
        total += to_offset(partial_value, offset)

    weight_rows = rest_weight()
    last_rows = after(later_rows, total)
    own += own_product(last_rows, model_width // 2, model_width)
    for offset in offsets:
        late = to_offset(rest_of(offset, last_rows)[:, rest_cut:], offset)
        late, own = lax.optimization_barrier((late, own))
        for piece, piece_rows in (
            (early[offset - 1], weight_rows[:rest_cut]),
            (late, weight_rows[rest_cut:]),
        ):
            others[offset - 1] += jnp.dot(piece, piece_rows, preferred_element_type=jnp.float32)

    mine = jnp.arange(resident_adapters, dtype=jnp.int32)[:, None, None] == slot_adapter[None, None, :]
    shrunk = total.astype(jnp.bfloat16)
    spread = jnp.where(mine, shrunk[None], jnp.zeros((), jnp.bfloat16))
    correction = lax.dot_general(
        spread.reshape(resident_adapters * rank_width, slot_count),
        adapter_up_weight.reshape(resident_adapters * rank_width, column_block_width),
        (((0,), (0,)), ((), ())),
        preferred_element_type=jnp.float32,
    )
    correction = (correction * ADAPTER_SCALE).astype(jnp.bfloat16)
    returned = lax.all_to_all(
        correction.reshape(adapter_count, holder_slots, column_block_width),
        "adapter",
        split_axis=0,
        concat_axis=0,
        tiled=True,
    ).reshape(slot_count, column_block_width)

    owners = [(tensor_index - offset) % tensor_count for offset in range(tensor_count)]
    return finish(
        jnp.stack(owners).astype(jnp.int32),
        [owner_slots(offset)[:, None] for offset in range(tensor_count)],
        [column[:, None] for column in inverse],
        [own] + others,
        returned,
    )


def solution(mesh):
    in_specs = (
        P(("adapter", "tensor"), None),
        P(),
        P(None, "tensor"),
        P("adapter", "tensor", None),
        P("adapter", None, "tensor"),
        P("adapter", None),
    )
    out_specs = P("adapter", "tensor")
    return jax.shard_map(
        per_device, mesh=mesh, in_specs=in_specs, out_specs=out_specs, check_vma=False
    )
```

```python
import functools

import jax
import jax.numpy as jnp
from jax import lax
from jax.experimental import pallas as pl
from jax.experimental.pallas import tpu as pltpu
from jax.sharding import PartitionSpec as P

DRAFT = 4
DEST = 12


EPS = 1e-05
ADAPTER_SCALE = 2.0


def chunk_bounds(width):
    first = max(width * 7 // 32 // 128, 1) * 128
    second = first + max(width * 5 // 16 // 128, 1) * 128
    return [(0, first), (first, second), (second, width)]


def after(value, *earlier):
    return lax.optimization_barrier((value, *earlier))[0]


def onehot(row_of_column, rows):
    row = lax.broadcasted_iota(jnp.int32, (rows, row_of_column.shape[0]), 0)
    return (row == row_of_column[None, :]).astype(jnp.bfloat16)


def features(rows, start, width):
    return lax.dynamic_slice_in_dim(rows, start, width, 1)


def shrink_kernel(adapters, down_ref, sent_ref, earlier_ref, slot_adapter_ref, out_ref, total_ref):
    rank_width, slots = out_ref.shape
    step = 256 if slots % 256 == 0 else slots
    part = pl.program_id(0)

    @pl.when(part == 0)
    def _():
        total_ref[...] = earlier_ref[...]

    for start in range(0, slots, step):
        columns = slice(start, start + step)
        total_ref[:, columns] += lax.dot_general(
            down_ref[...],
            sent_ref[columns, :],
            (((1,), (1,)), ((), ())),
            preferred_element_type=jnp.float32,
        )

    @pl.when(part == pl.num_programs(0) - 1)
    def _():
        named = slot_adapter_ref[...]
        chosen = jnp.zeros((rank_width, slots), jnp.float32)
        for adapter in range(adapters):
            rows = total_ref[adapter * rank_width : (adapter + 1) * rank_width, :]
            chosen = jnp.where(named == adapter, rows, chosen)
        out_ref[...] = chosen


def shrink_last(down, sent, earlier, slot_adapter, adapters):
    rows, width = down.shape
    slots = sent.shape[0]
    tile = next(size for size in (640, 512, 384, 256, 128) if width % size == 0)
    return pl.pallas_call(
        functools.partial(shrink_kernel, adapters),
        out_shape=jax.ShapeDtypeStruct((rows // adapters, slots), jnp.float32),
        grid=(width // tile,),
        in_specs=[
            pl.BlockSpec((rows, tile), lambda k: (0, k)),
            pl.BlockSpec((slots, tile), lambda k: (0, k)),
            pl.BlockSpec((rows, slots), lambda k: (0, 0)),
            pl.BlockSpec((1, slots), lambda k: (0, 0)),
        ],
        out_specs=pl.BlockSpec((rows // adapters, slots), lambda k: (0, 0)),
        scratch_shapes=[pltpu.VMEM((rows, slots), jnp.float32)],
        compiler_params=pltpu.CompilerParams(vmem_limit_bytes=20 * 1024 * 1024),
        cost_estimate=pl.CostEstimate(
            flops=2 * rows * width * slots,
            bytes_accessed=(rows + slots) * width * 2 + rows * slots * 4,
            transcendentals=0,
        ),
    )(down, sent, earlier, slot_adapter)


def finish_kernel(count, owners_ref, *refs):
    slots, factors, bases = refs[:count], refs[count : 2 * count], refs[2 * count : 3 * count]
    returned_ref, out_ref = refs[3 * count :]
    rows, width = bases[0].shape
    half = returned_ref.shape[1]

    def place(i):
        return pl.ds(pl.multiple_of(owners_ref[i] * rows, rows), rows)

    def keys():
        for i in range(count):
            out_ref[place(i), :half] = (bases[i][:, :half] * factors[i][...]).astype(out_ref.dtype)

    def vals():
        for i in range(count):
            slot = lax.broadcasted_iota(jnp.int32, (rows, returned_ref.shape[0]), 1)
            take = jnp.where(slot == slots[i][...], 1.0, 0.0).astype(jnp.bfloat16)
            delta = jnp.dot(take, returned_ref[...], preferred_element_type=jnp.float32)
            value = (bases[i][:, width - half :] + delta) * factors[i][...]
            out_ref[place(i), width - half :] = value.astype(out_ref.dtype)

    if width == half:
        pl.when(pl.program_id(0) == 0)(keys)
        pl.when(pl.program_id(0) == 1)(vals)
    else:
        keys()
        vals()


def finish(owners, slots, factors, bases, returned):
    count = len(bases)
    rows, width = bases[0].shape
    block = width // 2 if width // 2 % 128 == 0 else width
    whole = lambda shape: pl.BlockSpec(shape, lambda j: (0, 0))
    return pl.pallas_call(
        functools.partial(finish_kernel, count),
        out_shape=jax.ShapeDtypeStruct((rows * count, width), jnp.bfloat16),
        grid=(width // block,),
        in_specs=[pl.BlockSpec(memory_space=pltpu.SMEM)]
        + [whole((rows, 1))] * (2 * count)
        + [pl.BlockSpec((rows, block), lambda j: (0, j))] * count
        + [whole(returned.shape)],
        out_specs=pl.BlockSpec((rows * count, block), lambda j: (0, j)),
        compiler_params=pltpu.CompilerParams(vmem_limit_bytes=20 * 1024 * 1024),
        cost_estimate=pl.CostEstimate(
            flops=2 * rows * count * returned.shape[0] * returned.shape[1],
            bytes_accessed=rows * count * width * 6 + returned.size * 2,
            transcendentals=0,
        ),
    )(owners, *slots, *factors, *bases, returned)


def per_device(
    residual_rows,
    norm_gain_vector,
    key_value_weight,
    adapter_down_weight,
    adapter_up_weight,
    request_adapter_index,
):
    tensor_count = lax.axis_size("tensor")
    tensor_index = lax.axis_index("tensor")
    adapter_count = lax.axis_size("adapter")
    adapter_index = lax.axis_index("adapter")
    own_tokens, model_width = residual_rows.shape
    share_width = model_width // tensor_count
    column_block_width = adapter_up_weight.shape[2]
    resident_adapters = adapter_down_weight.shape[0]
    rank_width = adapter_down_weight.shape[2]
    holder_slots = DEST * DRAFT
    slot_count = adapter_count * holder_slots
    offsets = range(1, tensor_count)

    def to_offset(value, offset):
        pairs = [(i, (i + offset) % tensor_count) for i in range(tensor_count)]
        return lax.ppermute(value, "tensor", pairs)

    request_ids = request_adapter_index[:, 0]
    request_count = request_ids.shape[0]
    holder = request_ids // resident_adapters
    position = lax.broadcasted_iota(jnp.int32, (request_count, request_count), 0)
    earlier = lax.broadcasted_iota(jnp.int32, (request_count, request_count), 1) < position
    same = holder[:, None] == holder[None, :]
    ranking = jnp.sum((same & earlier).astype(jnp.int32), axis=1)
    request_slot = holder * DEST + ranking
    draft_steps = jnp.arange(DRAFT, dtype=jnp.int32)[None, :]
    token_slot = (request_slot[:, None] * DRAFT + draft_steps).reshape(-1)

    slot = lax.broadcasted_iota(jnp.int32, (adapter_count * DEST, request_count), 0)
    hit = slot == request_slot[None, :]
    local = request_ids - holder * resident_adapters
    slot_local = jnp.sum(jnp.where(hit, local[None, :] + 1, 0), axis=1) - 1
    told = lax.all_to_all(
        slot_local.reshape(adapter_count, DEST), "adapter", split_axis=0, concat_axis=0, tiled=True
    )
    slot_adapter = jnp.repeat(told.reshape(-1), DRAFT)

    def owner_slots(offset):
        owner = (tensor_index - offset) % tensor_count
        return lax.dynamic_slice_in_dim(token_slot, owner * own_tokens, own_tokens, 0)

    place = [onehot(owner_slots(offset), slot_count) for offset in range(tensor_count)]

    def scaled(rows, start, width):
        gain = lax.dynamic_slice_in_dim(norm_gain_vector, start, width, 0).astype(jnp.float32)
        return (features(rows, start, width).astype(jnp.float32) * gain).astype(jnp.bfloat16)

    down = jnp.swapaxes(adapter_down_weight, 1, 2).reshape(resident_adapters * rank_width, share_width)
    others = [jnp.zeros((own_tokens, 2 * column_block_width), jnp.float32) for _ in offsets]
    own_start = tensor_index * share_width
    bounds = chunk_bounds(share_width)

    def to_send(rows, low, width):
        starts = [(tensor_index + offset) % tensor_count * share_width + low for offset in offsets]
        return [scaled(rows, start, width) for start in starts]

    def rest_of(offset, rows):
        target = (tensor_index + offset) % tensor_count
        rest = [scaled(rows, (target + j) % tensor_count * share_width, share_width) for j in offsets]
        return jnp.concatenate(rest, axis=1)

    def rest_weight():
        starts = [(tensor_index + j) % tensor_count * share_width for j in offsets]
        return jnp.concatenate(
            [lax.dynamic_slice_in_dim(key_value_weight, start, share_width, 0) for start in starts], axis=0
        )

    def own_product(rows, low, high):
        return jnp.dot(
            scaled(rows, low, high - low), key_value_weight[low:high], preferred_element_type=jnp.float32
        )

    later_rows = after(residual_rows, slot_local)
    parts = len(bounds)
    rest_width = model_width - share_width
    rest_cut = max(rest_width * 13 // 16 // 128, 1) * 128
    sending = [
        to_send(residual_rows if part == 0 else later_rows, low, high - low)
        for part, (low, high) in enumerate(bounds)
    ]
    own, inverse, gate = None, [], ()
    partials = []
    count = len(offsets)
    for part, (low, high) in enumerate(bounds):
        width = high - low
        sending[part] = [after(piece, *gate) for piece in sending[part]]
        pieces = [to_offset(piece, offset) for offset, piece in zip(offsets, sending[part])]
        outgoing = jnp.dot(
            place[0],
            scaled(residual_rows if part == 0 else later_rows, own_start + low, width),
            preferred_element_type=jnp.float32,
        ).astype(jnp.bfloat16)
        outgoing = lax.optimization_barrier(outgoing).astype(jnp.float32)
        if part == 0:
            pieces = [after(piece, told) for piece in pieces]
        elif part == 1:
            values = after(later_rows, *gate).astype(jnp.float32)
            inverse = [lax.rsqrt(jnp.mean(values * values, axis=-1) + EPS)]
            inverse += [to_offset(inverse[0], offset) for offset in offsets]
            own = own_product(after(later_rows, *gate), 0, model_width // 4)
            own, *pieces = lax.optimization_barrier((own, *pieces, inverse[0]))[: count + 1]
        else:
            own += own_product(after(later_rows, *gate), model_width // 4, model_width * 3 // 4)
            own, *pieces = lax.optimization_barrier((own, *pieces))
        gate = pieces
        for offset, piece in zip(offsets, pieces):
            outgoing += jnp.dot(place[offset], piece, preferred_element_type=jnp.float32)
            others[offset - 1] += jnp.dot(
                piece,
                lax.dynamic_slice_in_dim(key_value_weight, own_start + low, width, 0),
                preferred_element_type=jnp.float32,
            )
        outgoing = outgoing.astype(jnp.bfloat16).reshape(adapter_count, holder_slots, width)
        sent = lax.all_to_all(outgoing, "adapter", split_axis=0, concat_axis=0, tiled=True)
        sent = sent.reshape(slot_count, width)
        if part < parts - 1:
            if partials:
                sent = after(sent, partials[-1])
            partial_value = lax.dot_general(
                down[:, low:high], sent, (((1,), (1,)), ((), ())), preferred_element_type=jnp.float32
            )
            partials.append(partial_value + partials[-1] if partials else partial_value)

    early = [
        to_offset(after(rest_of(offset, later_rows)[:, :rest_cut], *gate), offset) for offset in offsets
    ]
    low, high = bounds[-1]
    sent, earlier_sum, last_down, *tied = lax.optimization_barrier(
        (sent, partials[-1], down[:, low:high], *others, *inverse[1:], *early)
    )
    others, inverse[1:], early = tied[:count], tied[count : 2 * count], tied[2 * count :]
    partial_value = shrink_last(last_down, sent, earlier_sum, slot_adapter[None, :], resident_adapters)
    total = partial_value
    for offset in offsets:
        total += to_offset(partial_value, offset)

    weight_rows = rest_weight()
    last_rows = after(later_rows, total)
    own += own_product(last_rows, model_width * 3 // 4, model_width)
    early = [after(piece, total) for piece in early]
    for offset in offsets:
        late = to_offset(rest_of(offset, last_rows)[:, rest_cut:], offset)
        late, own = lax.optimization_barrier((late, own))
        for piece, piece_rows in (
            (early[offset - 1], weight_rows[:rest_cut]),
            (late, weight_rows[rest_cut:]),
        ):
            others[offset - 1] += jnp.dot(piece, piece_rows, preferred_element_type=jnp.float32)

    mine = jnp.arange(resident_adapters, dtype=jnp.int32)[:, None, None] == slot_adapter[None, None, :]
    shrunk = total.astype(jnp.bfloat16)
    spread = jnp.where(mine, shrunk[None], jnp.zeros((), jnp.bfloat16))
    correction = lax.dot_general(
        spread.reshape(resident_adapters * rank_width, slot_count),
        adapter_up_weight.reshape(resident_adapters * rank_width, column_block_width),
        (((0,), (0,)), ((), ())),
        preferred_element_type=jnp.float32,
    )
    correction = (correction * ADAPTER_SCALE).astype(jnp.bfloat16)
    returned = lax.all_to_all(
        correction.reshape(adapter_count, holder_slots, column_block_width),
        "adapter",
        split_axis=0,
        concat_axis=0,
        tiled=True,
    ).reshape(slot_count, column_block_width)

    owners = [(tensor_index - offset) % tensor_count for offset in range(tensor_count)]
    return finish(
        jnp.stack(owners).astype(jnp.int32),
        [owner_slots(offset)[:, None] for offset in range(tensor_count)],
        [column[:, None] for column in inverse],
        [own] + others,
        returned,
    )


def solution(mesh):
    in_specs = (
        P(("adapter", "tensor"), None),
        P(),
        P(None, "tensor"),
        P("adapter", "tensor", None),
        P("adapter", None, "tensor"),
        P("adapter", None),
    )
    out_specs = P("adapter", "tensor")
    return jax.shard_map(
        per_device, mesh=mesh, in_specs=in_specs, out_specs=out_specs, check_vma=False
    )
```
